32 devices in a mesh: blk: 8 (over z, y), kv: 4 (over x, core).
Axes of the slice: x: 2, y: 2, z: 4, core: 2. Of those that a mesh axis runs over, the one named last changes fastest.
Arguments:
- queries: bfloat16 [2048, 16, 2, 128], P('blk', 'kv'), may hold values from -80 to 80
- suffix_kv: bfloat16 [2048, 2, 16, 128], P('blk', None, 'kv'), may hold values from -4 to 4
- cache: bfloat16 [16, 2, 32, 16, 128], P('blk', None, None, 'kv'), may hold values from -4 to 4
- page_table: int32 [16], replicated, may hold values from 0 to 15, each once
- req_prefix: int32 [32], P('blk'), may hold values from 0 to 3
- suffix_len: int32 [8, 4], P('blk'), may hold values from 1 to 128, 256 in all within a row
- att_experts: int32 [2048, 2], P('blk'), may hold values from 0 to 7, all different within a row
- att_gates: float32 [2048, 2], P('blk'), may hold values from 0.2 to 1
- out_proj: bfloat16 [8, 2048, 2048], P(None, 'blk', 'kv'), may hold values from -0.375 to 0.375
Outputs:
- attn_out: bfloat16 [2048, 2048], P('blk', 'kv')
The draws below stay inside these ranges and needn't reach their ends.
Inputs may be any that keep to these rules, and one draw needn't show every extreme that they name: `page_table`: every physical page holds exactly one page of one prefix. `suffix_len`: each row adds up to 256, so requests never span two indices of blk; the longest suffix of each row is exactly 128. `att_experts`: the experts of one token differ.
All inputs are finite; a program needn't handle non-finite values.
Results may differ from the reference program's by a relative error of at most 0.015.
Values may be sent and summed in bfloat16 or wider, within the bound.
A program may use at most 128 MiB of HBM per device.

```python
import math
import jax
import jax.numpy as jnp
import numpy as np
from jax import lax

D = 2048
KVH = 16
HD = 128
E_ATT = 8
TOPA = 2
PAGE = 32
PREFIXES = 4
REQ_DEV = 4
TOK_DEV = 256
TOKENS = 2048
NPAGES = 16
REQS = 32
SUFMOST = 128
N_BLK = 8


def shared_keys(key):
    return jnp.clip(jax.random.normal(jax.random.fold_in(key, 7), (TOKENS, KVH, HD), jnp.float32), -4.0, 4.0)


def draw_suffix_kv(key, part):
    key_field = shared_keys(key)
    value_field = jnp.clip(jax.random.normal(jax.random.fold_in(key, 9), (TOKENS, KVH, HD), jnp.float32), -4.0, 4.0)
    return jnp.stack([key_field, value_field], axis=1).astype(jnp.bfloat16)


def draw_queries(key, part):
    drawn = jnp.clip(2.0 * jax.random.normal(jax.random.fold_in(key, 3), (TOKENS, KVH, TOPA, HD), jnp.float32), -8.0, 8.0)
    return drawn.astype(jnp.bfloat16)


def touch_ends(values, key, low, top_value):
    longest = values.shape.index(max(values.shape))
    spots = []
    for shift in (0, 1):
        where = [jax.random.randint(jax.random.fold_in(key, axis), (), 0, length) for axis, length in enumerate(values.shape)]
        where[longest] = (where[longest] + shift) % values.shape[longest]
        spots.append(tuple(where))
    return values.at[spots[0]].set(low).at[spots[1]].set(top_value)


def shard_levels(rng, extent, cuts, low, high):
    def one(position, shards_of):
        draws = jax.random.uniform(jax.random.fold_in(jax.random.fold_in(rng, 6), position), (shards_of,), jnp.float32, low / len(cuts), high / len(cuts))
        return jnp.repeat(jnp.exp(draws), extent[position] // shards_of).reshape((-1,) + (1,) * (len(extent) - position - 1))

    gain = one(*cuts[0])
    for cut in cuts[1:]:
        gain = gain * one(*cut)
    return gain


def cumulative_ranks(amount, skew):
    portions = [(1 << 20) // math.isqrt(standing ** skew) + 1 for standing in range(1, amount + 1)]
    scale = 1 + sum(portions) // (1 << 30)
    return np.cumsum(np.array([max(1, weight // scale) for weight in portions]))


def ranked(own_key, shape, amount, skew):
    table = cumulative_ranks(amount, skew)
    lot = jax.random.randint(jax.random.fold_in(own_key, 1), shape, 0, int(table[amount - 1]))
    rank = jnp.searchsorted(jnp.asarray(table, jnp.int32), lot, side="right")
    return jax.random.permutation(jax.random.fold_in(own_key, 2), amount)[rank].astype(jnp.int32)


def picks_of(own_key, rows, amount, top, lift):
    order = jax.random.permutation(jax.random.fold_in(own_key, 1), amount)
    pull = order
    for power in range(3):
        pull = pull * pull // amount
    pull = pull * lift // amount
    chance = jax.random.randint(jax.random.fold_in(own_key, 2), (rows, amount), 0, 4096) + pull
    sure = jax.random.permutation(jax.random.fold_in(own_key, 3), rows)[jnp.arange(amount) % rows]
    chance = jnp.where(jnp.arange(rows)[:, None] == sure[None, :], 1 << 14, chance)
    merit = chance * amount + jnp.arange(amount)
    return lax.top_k(merit.astype(jnp.int32), top)[1].astype(jnp.int32)


def split_up(count, total, most, skew):
    portions = [(1 << 20) // math.isqrt(standing ** skew) + 1 for standing in range(2, count + 1)]
    rest, holding = total - most - (count - 1), [1] * (count - 1)
    while rest > 0:
        free = [i for i in range(count - 1) if holding[i] < most]
        pool, remaining = sum([portions[i] for i in free]), rest
        for i in free:
            more = min(most - holding[i], max(1, remaining * portions[i] // pool), rest)
            holding[i] = holding[i] + more
            rest = rest - more
    return np.array([most] + holding)


def uneven_parts(key, count, total, most, slope):
    if count == 2:
        one = jax.random.randint(key, (), max(1, total - most), min(most, total - 1) + 1)
        return jnp.stack([one, total - one])
    sizes = jnp.asarray(split_up(count, total, most, slope), jnp.int32)
    pairs = (count - 1) // 2
    source_of, taker = sizes[1:1 + 2 * pairs:2], sizes[2:2 + 2 * pairs:2]
    room = jnp.minimum(source_of - 1, most - taker)
    moved = jax.random.randint(jax.random.fold_in(key, 1), (pairs,), 0, 1 << 20) % (room + 1)
    sizes = sizes.at[1:1 + 2 * pairs:2].set(source_of - moved).at[2:2 + 2 * pairs:2].set(taker + moved)
    return sizes[jax.random.permutation(jax.random.fold_in(key, 2), count)]


def centred(key, dims, deviation, limit, split=(), held_as=jnp.bfloat16):
    array = jax.random.normal(key, dims, jnp.float32) * deviation
    if len(split) > 0:
        array = shard_levels(key, dims, split, -0.22, 0.18) * array
    return jnp.clip(array, min=-limit, max=limit).astype(held_as)


def setup_inputs(seed: int = 0) -> dict:
    key_list = jax.random.split(jax.random.key(seed), 10)
    queries = draw_queries(jax.random.fold_in(key_list[9], 71), 0)
    suffix_kv = draw_suffix_kv(jax.random.fold_in(key_list[9], 71), 0)
    cache = centred(key_list[2], (NPAGES, 2, PAGE, KVH, HD), 1.0, 4.0, ((0, 8), (3, 4)))
    page_table = jax.random.permutation(key_list[3], NPAGES).astype(jnp.int32)
    req_prefix = touch_ends(ranked(key_list[4], (REQS,), PREFIXES, 2), jax.random.fold_in(key_list[4], 3), 0, PREFIXES - 1).astype(jnp.int32)
    suffix_len = jax.vmap(lambda own: uneven_parts(own, REQ_DEV, TOK_DEV, SUFMOST, 2))(jax.random.split(key_list[5], N_BLK)).reshape((N_BLK, REQ_DEV)).astype(jnp.int32)
    att_experts = picks_of(key_list[6], TOKENS, E_ATT, TOPA, 2048)
    att_gates = jnp.clip(0.2 + 0.8 * jax.random.uniform(key_list[7], (TOKENS, TOPA), jnp.float32) ** shard_levels(key_list[7], (TOKENS, TOPA), ((0, 8),), -0.2, 0.2), 0.2, 1.0)
    out_proj = centred(key_list[8], (E_ATT, D, KVH * HD), (KVH * HD // 8) ** -0.5, 0.375, ((1, 8), (2, 4)))
    return dict(queries=queries, suffix_kv=suffix_kv, cache=cache, page_table=page_table, req_prefix=req_prefix, suffix_len=suffix_len, att_experts=att_experts, att_gates=att_gates, out_proj=out_proj)


MASKED_SCORE = -1e+30

def reference(queries, suffix_kv, cache, page_table, req_prefix, suffix_len, att_experts, att_gates, out_proj):
    total_pages = page_table.shape[0]
    per_prefix = total_pages // PREFIXES
    page_ids = jnp.arange(total_pages, dtype=jnp.int32)
    page_prefix = lax.optimization_barrier(jnp.sum(jnp.where(page_table[None, :] == page_ids[:, None], (page_ids // per_prefix)[None, :], 0), axis=1)).astype(jnp.int32)
    key_prefix = jnp.repeat(page_prefix, PAGE)
    cache_keys = cache[:, 0].reshape(total_pages * PAGE, KVH, HD)
    cache_values = cache[:, 1].reshape(total_pages * PAGE, KVH, HD)
    scaling = 1.0 / math.sqrt(HD)
    weights_full = out_proj.astype(jnp.float32)
    expert_ids = jnp.arange(E_ATT, dtype=jnp.int32)
    positions = jnp.arange(TOK_DEV, dtype=jnp.int32)
    request_ids = jnp.arange(REQ_DEV, dtype=jnp.int32)

    def one_block(block_index):
        offset = block_index * TOK_DEV
        query_rows = lax.dynamic_slice_in_dim(queries, offset, TOK_DEV, 0)
        own_rows = lax.dynamic_slice_in_dim(suffix_kv, offset, TOK_DEV, 0)
        lengths = lax.dynamic_slice_in_dim(suffix_len, block_index, 1, 0)[0]
        prefix_ids = lax.dynamic_slice_in_dim(req_prefix, block_index * REQ_DEV, REQ_DEV, 0)
        expert_rows = lax.dynamic_slice_in_dim(att_experts, offset, TOK_DEV, 0)
        gate_rows = lax.dynamic_slice_in_dim(att_gates, offset, TOK_DEV, 0)
        request_ends = jnp.cumsum(lengths)
        request_of = lax.optimization_barrier(jnp.sum((positions[:, None] >= request_ends[None, :]).astype(jnp.int32), axis=1))
        token_prefix = lax.optimization_barrier(jnp.sum(jnp.where(request_of[:, None] == request_ids[None, :], prefix_ids[None, :], 0), axis=1))
        prefix_ok = token_prefix[:, None] == key_prefix[None, :]
        suffix_ok = (request_of[:, None] == request_of[None, :]) & (positions[:, None] >= positions[None, :])
        allowed = jnp.concatenate([prefix_ok, suffix_ok], axis=1)

        def one_head(head_index):
            head_queries = query_rows[:, head_index].astype(jnp.float32)
            head_keys = jnp.concatenate([cache_keys[:, head_index], own_rows[:, 0, head_index]], axis=0).astype(jnp.float32)
            head_values = jnp.concatenate([cache_values[:, head_index], own_rows[:, 1, head_index]], axis=0).astype(jnp.float32)
            scores = jnp.einsum('tjd,kd->tjk', head_queries, head_keys) * scaling
            scores = jnp.where(allowed[:, None, :], scores, MASKED_SCORE)
            row_max = lax.optimization_barrier(jnp.max(scores, axis=2, keepdims=True))
            weights = jnp.where(allowed[:, None, :], jnp.exp(scores - row_max), 0.0)
            denominator = lax.optimization_barrier(jnp.sum(weights, axis=2))
            rounded = lax.optimization_barrier(weights.astype(jnp.bfloat16)).astype(jnp.float32)
            numerator = jnp.einsum('tjk,kd->tjd', rounded, head_values)
            return (numerator / denominator[..., None]).astype(jnp.bfloat16)
        attention = jnp.moveaxis(lax.map(one_head, jnp.arange(KVH, dtype=jnp.int32)), 0, 1)
        gate_table = jnp.where(expert_rows[:, :, None] == expert_ids[None, None, :], gate_rows[:, :, None], 0.0)
        combined = jnp.zeros((E_ATT, TOK_DEV, KVH, HD), jnp.float32)
        for slot_index in range(TOPA):
            combined = combined + gate_table[:, slot_index, :].T[:, :, None, None] * attention[:, :, slot_index, :].astype(jnp.float32)[None]
        combined = combined.reshape(E_ATT, TOK_DEV, KVH * HD).astype(jnp.bfloat16)
        combined = lax.optimization_barrier(combined).astype(jnp.float32)
        return jnp.einsum('etf,ecf->tc', combined, weights_full).astype(jnp.bfloat16)
    blocks_out = lax.map(one_block, jnp.arange(TOKENS // TOK_DEV, dtype=jnp.int32))
    return blocks_out.reshape(TOKENS, D)
```

```python
import functools
import math

import jax
import jax.numpy as jnp
from jax import lax
from jax.experimental import pallas as pl
from jax.experimental.pallas import tpu as pltpu
from jax.sharding import PartitionSpec as P

PREFIXES = 4


MASKED_SCORE = -1e30


def absorb(carried, query_rows, key_rows, value_rows, allowed):
    running_max, denominator, numerator = carried
    scaling = 1.0 / math.sqrt(query_rows.shape[-1])
    scores = (
        jnp.einsum("thjd,khd->thjk", query_rows, key_rows, preferred_element_type=jnp.float32)
        * scaling
    )
    visible = allowed[:, None, None, :]
    scores = jnp.where(visible, scores, MASKED_SCORE)
    new_max = jnp.maximum(running_max, jnp.max(scores, axis=3))
    weights = jnp.where(visible, jnp.exp(scores - new_max[..., None]), 0.0)
    factor = jnp.exp(running_max - new_max)
    denominator = denominator * factor + jnp.sum(weights, axis=3)
    numerator = numerator * factor[..., None] + jnp.einsum(
        "thjk,khd->thjd",
        weights.astype(jnp.bfloat16),
        value_rows,
        preferred_element_type=jnp.float32,
    )
    return (new_max, denominator, numerator)


def body(
    queries, suffix_kv, cache, page_table, req_prefix, suffix_len, att_experts, att_gates, out_proj
):
    tok_count = queries.shape[0]
    head_count = queries.shape[1]
    slot_count = queries.shape[2]
    head_width = queries.shape[3]
    page_rows = cache.shape[2]
    total_pages = page_table.shape[0]
    per_prefix = total_pages // PREFIXES
    page_ids = jnp.arange(total_pages, dtype=jnp.int32)
    owner_match = page_table[None, :] == page_ids[:, None]
    page_prefix = jnp.sum(jnp.where(owner_match, (page_ids // per_prefix)[None, :], 0), axis=1)
    lengths = suffix_len[0]
    request_ends = jnp.cumsum(lengths)
    positions = jnp.arange(tok_count, dtype=jnp.int32)
    request_of = jnp.sum((positions[:, None] >= request_ends[None, :]).astype(jnp.int32), axis=1)
    request_ids = jnp.arange(lengths.shape[0], dtype=jnp.int32)
    token_prefix = jnp.sum(
        jnp.where(request_of[:, None] == request_ids[None, :], req_prefix[None, :], 0), axis=1
    )
    own_keys = suffix_kv[:, 0]
    own_values = suffix_kv[:, 1]
    block_rows = min(tok_count, 512)
    blocks = tok_count // block_rows

    def suffix_block(block_index):
        allowed = (request_of[:, None] == request_of[None, :]) & (
            positions[:, None] >= positions[None, :]
        )
        initial = (
            jnp.full((block_rows, head_count, slot_count), MASKED_SCORE, jnp.float32),
            jnp.zeros((block_rows, head_count, slot_count), jnp.float32),
            jnp.zeros((block_rows, head_count, slot_count, head_width), jnp.float32),
        )
        return absorb(initial, queries, own_keys, own_values, allowed)

    first_max, first_sum, first_acc = lax.map(suffix_block, jnp.arange(blocks, dtype=jnp.int32))
    carried = (
        first_max.reshape(tok_count, head_count, slot_count),
        first_sum.reshape(tok_count, head_count, slot_count),
        first_acc.reshape(tok_count, head_count, slot_count, head_width),
    )
    key_cap = max(1, 256 // page_rows)
    page_piece = lax.all_gather(cache, "blk", axis=0, tiled=True)
    number = page_piece.shape[0]
    pages_tile = 1
    for candidate in range(1, min(number, key_cap) + 1):
        if number % candidate == 0:
            pages_tile = candidate
    tile_owners = page_prefix.reshape(number // pages_tile, pages_tile)
    page_tiles = page_piece.reshape(
        number // pages_tile, pages_tile, 2, page_rows, head_count, head_width
    )

    def absorb_tile(current, tile_item):
        one_tile, tile_owner = tile_item
        tile_keys = one_tile[:, 0].reshape(pages_tile * page_rows, head_count, head_width)
        tile_values = one_tile[:, 1].reshape(pages_tile * page_rows, head_count, head_width)
        key_prefix = jnp.repeat(tile_owner, page_rows)
        allowed = token_prefix[:, None] == key_prefix[None, :]
        updated = absorb(current, queries, tile_keys, tile_values, allowed)
        return (updated, None)

    finished, ignored = lax.scan(absorb_tile, carried, (page_tiles, tile_owners))
    running_max, denominator, numerator = finished
    attention = (numerator / denominator[..., None]).astype(jnp.bfloat16)
    expert_count = out_proj.shape[0]
    expert_ids = jnp.arange(expert_count, dtype=jnp.int32)
    gate_table = jnp.where(
        att_experts[:, :, None] == expert_ids[None, None, :], att_gates[:, :, None], 0.0
    )
    combined = jnp.zeros((expert_count, tok_count, head_count, head_width), jnp.float32)
    for slot_index in range(slot_count):
        combined = (
            combined
            + gate_table[:, slot_index, :].T[:, :, None, None]
            * attention[:, :, slot_index, :].astype(jnp.float32)[None]
        )
    combined = combined.reshape(expert_count, tok_count, head_count * head_width).astype(
        jnp.bfloat16
    )
    column_sums = jnp.einsum(
        "etf,ecf->tc",
        combined,
        lax.all_gather(out_proj, "blk", axis=1, tiled=True),
        preferred_element_type=jnp.float32,
    )
    return lax.psum_scatter(column_sums.astype(jnp.bfloat16), "kv", scatter_dimension=1, tiled=True)


MESH = pl.DeviceIdType.MESH
F32 = jnp.float32
BF16 = jnp.bfloat16
NT = (((1,), (1,)), ((), ()))


def fused_kernel(
    pt_ref, rp_ref, sl_ref, ex_ref, ga_ref, q_ref, s_ref, c_ref, w_ref, o_ref,
    cbuf, wbuf, ubuf, tbl, bias, comb, pbuf, prec, fin,
    loc_sem, cz_send, cz_recv, cy_send, cy_recv, w_send, w_recv,
    t_send, t_recv, u_send, u_recv, p_send, p_recv, o_send, o_recv,
):
    blk = lax.axis_index("blk")
    k = lax.axis_index("kv")
    z = blk // 2
    y = blk % 2
    heads = 4
    tok = q_ref.shape[0]
    cached = cbuf.shape[0] * cbuf.shape[1] * cbuf.shape[3]
    page_rows = cbuf.shape[3]
    pages = pt_ref.shape[0]
    reqs = rp_ref.shape[0]
    partner = z * 2 + (1 - y)

    def zpeer(d):
        return lax.rem(z + d, 4)

    barrier = pltpu.get_barrier_semaphore()
    for dz in range(4):
        for dk in range(4):
            if dz or dk:
                pl.semaphore_signal(
                    barrier, inc=1, device_id=(zpeer(dz) * 2 + y, lax.rem(k + dk, 4)), device_id_type=MESH
                )
    pl.semaphore_signal(barrier, inc=1, device_id=(partner, k), device_id_type=MESH)
    pl.semaphore_wait(barrier, 16)

    def remote(src, dst, send, recv, to):
        return pltpu.make_async_remote_copy(
            src_ref=src, dst_ref=dst, send_sem=send, recv_sem=recv, device_id=to, device_id_type=MESH
        )

    def cz(d, slot):
        return remote(c_ref, cbuf.at[slot], cz_send.at[d - 1], cz_recv.at[d - 1], (zpeer(d) * 2 + y, k))

    def cy(d):
        slot = lax.rem(z - d + 4, 4) * 2 + y
        source = c_ref if d == 0 else cbuf.at[slot]
        return remote(source, cbuf.at[slot], cy_send.at[d], cy_recv.at[d], (partner, k))

    for d in (1, 3, 2):
        cz(d, blk).start()
    cy(0).start()
    own_c = pltpu.make_async_copy(c_ref, cbuf.at[blk], loc_sem.at[0])
    own_c.start()
    own_w = pltpu.make_async_copy(w_ref, wbuf.at[0], loc_sem.at[1])
    own_w.start()

    lane = lax.broadcasted_iota(jnp.int32, (tok, 128), 1)
    hot0 = jnp.where(lane == ex_ref[:, 0:1], 1.0, 0.0)
    hot1 = jnp.where(lane - 8 == ex_ref[:, 1:2], 1.0, 0.0)
    hot = jnp.where(lane < 8, hot0, jnp.where(lane < 16, hot1, 0.0))
    tbl[z] = hot.T[0:16].astype(BF16)

    def tcopy(d, slot):
        return remote(tbl.at[slot], tbl.at[slot], t_send.at[d - 1], t_recv.at[d - 1], (zpeer(d) * 2 + y, k))

    row = lax.broadcasted_iota(jnp.int32, (tok, 128), 0)
    colq = lax.broadcasted_iota(jnp.int32, (8, tok), 1)
    req_row = jnp.zeros((tok, 128), jnp.int32)
    req_col = jnp.zeros((8, tok), jnp.int32)
    pref_row = jnp.full((tok, 128), rp_ref[0], jnp.int32)
    end = jnp.int32(0)
    for r in range(reqs):
        end = end + sl_ref[0, r]
        past = row >= end
        req_row = req_row + jnp.where(past, 1, 0)
        req_col = req_col + jnp.where(colq >= end, 1, 0)
        if r + 1 < reqs:
            pref_row = jnp.where(past, rp_ref[r + 1], pref_row)
    page_of = lax.broadcasted_iota(jnp.int32, (8, cached), 1) // page_rows
    key_prefix = jnp.zeros((8, cached), jnp.int32)
    for entry in range(pages):
        key_prefix = jnp.where(page_of == pt_ref[entry], entry // (pages // PREFIXES), key_prefix)
    bias[:, 0:cached] = jnp.where(pref_row[:, 0:1] == key_prefix[0:1, :], 0.0, MASKED_SCORE)
    keep = jnp.logical_and(req_row[:, 0:1] == req_col[0:1, :], row[:, 0:1] >= colq[0:1, :])
    bias[:, cached:] = jnp.where(keep, 0.0, MASKED_SCORE)

    for d in (1, 3, 2):
        cz(d, lax.rem(z - d + 4, 4) * 2 + y).wait_recv()
        cy(d).start()
    own_c.wait()

    def wcopy():
        return remote(w_ref, wbuf.at[1], w_send.at[0], w_recv.at[0], (partner, k))

    wcopy().start()
    for d in (1, 2, 3):
        tcopy(d, z).start()

    def ycopy_in(d):
        slot = lax.rem(z - d + 4, 4) * 2 + (1 - y)
        return remote(cbuf.at[slot], cbuf.at[slot], cy_send.at[d], cy_recv.at[d], (partner, k))

    for d in range(4):
        ycopy_in(d).wait_recv()

    def ucopy(h, d, slot):
        return remote(
            ubuf.at[slot, h], ubuf.at[slot, h], u_send.at[h, d - 1], u_recv.at[h, d - 1], (zpeer(d) * 2 + y, k)
        )

    factor = math.log2(math.e) / math.sqrt(128)
    for h in range(heads):
        span = slice(h * 128, (h + 1) * 128)
        keys = cbuf[:, :, 0, :, span].reshape(cached, 128)
        values = cbuf[:, :, 1, :, span].reshape(cached, 128)
        skeys = s_ref[:, span]
        svalues = s_ref[:, heads * 128 + h * 128 : heads * 128 + (h + 1) * 128]
        for j in range(2):
            place = slice((h * 2 + j) * 128, (h * 2 + j + 1) * 128)
            query = q_ref[:, place]
            sa = lax.dot_general(query, keys, NT, preferred_element_type=F32) * factor + bias[:, 0:cached]
            sb = lax.dot_general(query, skeys, NT, preferred_element_type=F32) * factor + bias[:, cached:]
            top = jnp.maximum(jnp.max(sa, axis=1, keepdims=True), jnp.max(sb, axis=1, keepdims=True))
            pa = jnp.exp2(sa - top)
            pb = jnp.exp2(sb - top)
            den = jnp.sum(pa, axis=1, keepdims=True) + jnp.sum(pb, axis=1, keepdims=True)
            num = jnp.dot(pa.astype(BF16), values, preferred_element_type=F32) + jnp.dot(
                pb.astype(BF16), svalues, preferred_element_type=F32
            )
            att = (num / den).astype(BF16).astype(F32)
            ubuf[z, h, :, j * 128 : (j + 1) * 128] = (att * ga_ref[:, j : j + 1]).astype(BF16)
        for d in (1, 3, 2):
            ucopy(h, d, z).start()
    own_w.wait()

    sel_row = lax.broadcasted_iota(jnp.int32, (16, 16 * 128), 0)
    sel_col = lax.broadcasted_iota(jnp.int32, (16, 16 * 128), 1) // 128
    select = jnp.where(sel_row == sel_col, 1.0, 0.0).astype(BF16)

    def pcopy(i, e):
        q = lax.rem(k + e, 4)
        rows = pl.ds(pl.multiple_of(q * 64, 64), 64)
        return remote(
            pbuf.at[i, rows], prec.at[i, e - 1], p_send.at[i, e - 1], p_recv.at[i, e - 1], (blk, q)
        )

    def half_of(i):
        half = jnp.where(i < 4, y, 1 - y)
        return pl.ds(pl.multiple_of(half * 256, 256), 256)

    def ocopy(i):
        d = lax.rem(i, 4)
        rows = pl.ds(pl.multiple_of(k * 64, 64), 64)
        to = lax.rem(z - d + 4, 4) * 2 + y
        return remote(fin.at[i], o_ref.at[rows, half_of(i)], o_send.at[i], o_recv.at[i // 4, k], (to, z))

    def step(i, carry):
        @pl.when(i < 8)
        def _():
            d = lax.rem(i, 4)
            source = lax.rem(z - d + 4, 4)

            @pl.when(i < 4)
            def _():
                @pl.when(d > 0)
                def _():
                    for h in range(heads):
                        remote(
                            ubuf.at[source, h], ubuf.at[source, h], u_send.at[h, d - 1], u_recv.at[h, d - 1], (blk, k)
                        ).wait_recv()
                    remote(tbl.at[source], tbl.at[source], t_send.at[d - 1], t_recv.at[d - 1], (blk, k)).wait_recv()

                mask = lax.dot_general(
                    tbl[source], select, (((0,), (0,)), ((), ())), preferred_element_type=F32
                ).astype(BF16)
                for h in range(heads):
                    u0 = ubuf[source, h, :, 0:128]
                    u1 = ubuf[source, h, :, 128:256]
                    for e in range(8):
                        comb[d, :, e * 512 + h * 128 : e * 512 + (h + 1) * 128] = (
                            u0 * mask[:, e * 128 : (e + 1) * 128] + u1 * mask[:, (8 + e) * 128 : (9 + e) * 128]
                        )

            @pl.when(i == 4)
            def _():
                wcopy().wait_recv()

            part = jnp.zeros((tok, 256), F32)
            for e in range(8):
                part = part + lax.dot_general(
                    comb[d, :, e * 512 : (e + 1) * 512], wbuf[i // 4, e], NT, preferred_element_type=F32
                )
            pbuf[i] = part.astype(BF16)
            for e in (2, 3, 1):
                pcopy(i, e).start()

        @pl.when(i > 0)
        def _():
            p = i - 1
            own = pl.ds(pl.multiple_of(k * 64, 64), 64)
            total = pbuf[p, own].astype(F32)
            for e in (1, 2, 3):
                pcopy(p, e).wait_recv()
                total = total + prec[p, e - 1].astype(F32)
            here = jnp.logical_and(lax.rem(p, 4) == 0, k == z)

            @pl.when(here)
            def _():
                o_ref[own, half_of(p)] = total.astype(BF16)

            @pl.when(jnp.logical_not(here))
            def _():
                fin[p] = total.astype(BF16)
                ocopy(p).start()

        return carry

    lax.fori_loop(0, 9, step, 0)

    for g in range(2):
        for q in range(4):
            rows = pl.ds(q * 64, 64)

            @pl.when(jnp.logical_or(k != z, k != q))
            def _():
                remote(
                    fin.at[0], o_ref.at[rows, half_of(g * 4)], o_send.at[0], o_recv.at[g, q], (blk, k)
                ).wait_recv()

    def drain(i, carry):
        for e in (1, 2, 3):
            pcopy(i, e).wait_send()

        @pl.when(jnp.logical_or(lax.rem(i, 4) != 0, k != z))
        def _():
            ocopy(i).wait_send()

        return carry

    lax.fori_loop(0, 8, drain, 0)
    for d in (1, 2, 3):
        cz(d, blk).wait_send()
        tcopy(d, z).wait_send()
        for h in range(heads):
            ucopy(h, d, z).wait_send()
    for d in range(4):
        cy(d).wait_send()
    wcopy().wait_send()


def fused_body(
    queries, suffix_kv, cache, page_table, req_prefix, suffix_len, att_experts, att_gates, out_proj
):
    tok, heads, slots, width = queries.shape
    local_pages, _, page_rows = cache.shape[:3]
    experts, columns, features = out_proj.shape
    vmem = pl.BlockSpec(memory_space=pltpu.VMEM)
    smem = pl.BlockSpec(memory_space=pltpu.SMEM)
    dma = pltpu.SemaphoreType.DMA
    return pl.pallas_call(
        fused_kernel,
        out_shape=jax.ShapeDtypeStruct((tok, 2 * columns), BF16),
        in_specs=[smem, smem, smem, vmem, vmem, vmem, vmem, vmem, pl.BlockSpec(memory_space=pl.ANY)],
        out_specs=vmem,
        scratch_shapes=[
            pltpu.VMEM((8, local_pages, 2, page_rows, heads * width), BF16),
            pltpu.VMEM((2, experts, columns, features), BF16),
            pltpu.VMEM((4, heads, tok, slots * width), BF16),
            pltpu.VMEM((4, slots * experts, tok), BF16),
            pltpu.VMEM((tok, 8 * local_pages * page_rows + tok), F32),
            pltpu.VMEM((4, tok, experts * features), BF16),
            pltpu.VMEM((8, tok, columns), BF16),
            pltpu.VMEM((8, 3, tok // 4, columns), BF16),
            pltpu.VMEM((8, tok // 4, columns), BF16),
            dma((2,)), dma((3,)), dma((3,)), dma((4,)), dma((4,)), dma((1,)), dma((1,)),
            dma((3,)), dma((3,)), dma((heads, 3)), dma((heads, 3)),
            dma((8, 3)), dma((8, 3)), dma((8,)), dma((2, 4)),
        ],
        compiler_params=pltpu.CompilerParams(
            collective_id=0, has_side_effects=True, vmem_limit_bytes=48 * 1024 * 1024
        ),
        cost_estimate=pl.CostEstimate(flops=6 * 10**9, bytes_accessed=8 * 10**6, transcendentals=2 * 10**6),
    )(
        page_table, req_prefix, suffix_len, att_experts, att_gates,
        queries.reshape(tok, heads * slots * width),
        suffix_kv.reshape(tok, 2 * heads * width),
        cache.reshape(local_pages, 2, page_rows, heads * width),
        out_proj,
    )


def solution(mesh):
    in_specs = (
        P("blk", "kv", None, None),
        P("blk", None, "kv", None),
        P("blk", None, None, "kv", None),
        P(),
        P("blk"),
        P("blk", None),
        P("blk", None),
        P("blk", None),
        P(None, "blk", "kv"),
    )
    out_specs = P("blk", "kv")
    chosen = body
    if mesh.shape["blk"] == 2 * mesh.shape["kv"] and mesh.shape["kv"] == 4:
        chosen = fused_body
    return jax.shard_map(chosen, mesh=mesh, in_specs=in_specs, out_specs=out_specs, check_vma=False)
```

```python
import functools
import math

import jax
import jax.numpy as jnp
from jax import lax
from jax.experimental import pallas as pl
from jax.experimental.pallas import tpu as pltpu
from jax.sharding import PartitionSpec as P

PREFIXES = 4


MASKED_SCORE = -1e30


def absorb(carried, query_rows, key_rows, value_rows, allowed):
    running_max, denominator, numerator = carried
    scaling = 1.0 / math.sqrt(query_rows.shape[-1])
    scores = (
        jnp.einsum("thjd,khd->thjk", query_rows, key_rows, preferred_element_type=jnp.float32)
        * scaling
    )
    visible = allowed[:, None, None, :]
    scores = jnp.where(visible, scores, MASKED_SCORE)
    new_max = jnp.maximum(running_max, jnp.max(scores, axis=3))
    weights = jnp.where(visible, jnp.exp(scores - new_max[..., None]), 0.0)
    factor = jnp.exp(running_max - new_max)
    denominator = denominator * factor + jnp.sum(weights, axis=3)
    numerator = numerator * factor[..., None] + jnp.einsum(
        "thjk,khd->thjd",
        weights.astype(jnp.bfloat16),
        value_rows,
        preferred_element_type=jnp.float32,
    )
    return (new_max, denominator, numerator)


def body(
    queries, suffix_kv, cache, page_table, req_prefix, suffix_len, att_experts, att_gates, out_proj
):
    tok_count = queries.shape[0]
    head_count = queries.shape[1]
    slot_count = queries.shape[2]
    head_width = queries.shape[3]
    page_rows = cache.shape[2]
    total_pages = page_table.shape[0]
    per_prefix = total_pages // PREFIXES
    page_ids = jnp.arange(total_pages, dtype=jnp.int32)
    owner_match = page_table[None, :] == page_ids[:, None]
    page_prefix = jnp.sum(jnp.where(owner_match, (page_ids // per_prefix)[None, :], 0), axis=1)
    lengths = suffix_len[0]
    request_ends = jnp.cumsum(lengths)
    positions = jnp.arange(tok_count, dtype=jnp.int32)
    request_of = jnp.sum((positions[:, None] >= request_ends[None, :]).astype(jnp.int32), axis=1)
    request_ids = jnp.arange(lengths.shape[0], dtype=jnp.int32)
    token_prefix = jnp.sum(
        jnp.where(request_of[:, None] == request_ids[None, :], req_prefix[None, :], 0), axis=1
    )
    own_keys = suffix_kv[:, 0]
    own_values = suffix_kv[:, 1]
    block_rows = min(tok_count, 512)
    blocks = tok_count // block_rows

    def suffix_block(block_index):
        allowed = (request_of[:, None] == request_of[None, :]) & (
            positions[:, None] >= positions[None, :]
        )
        initial = (
            jnp.full((block_rows, head_count, slot_count), MASKED_SCORE, jnp.float32),
            jnp.zeros((block_rows, head_count, slot_count), jnp.float32),
            jnp.zeros((block_rows, head_count, slot_count, head_width), jnp.float32),
        )
        return absorb(initial, queries, own_keys, own_values, allowed)

    first_max, first_sum, first_acc = lax.map(suffix_block, jnp.arange(blocks, dtype=jnp.int32))
    carried = (
        first_max.reshape(tok_count, head_count, slot_count),
        first_sum.reshape(tok_count, head_count, slot_count),
        first_acc.reshape(tok_count, head_count, slot_count, head_width),
    )
    key_cap = max(1, 256 // page_rows)
    page_piece = lax.all_gather(cache, "blk", axis=0, tiled=True)
    number = page_piece.shape[0]
    pages_tile = 1
    for candidate in range(1, min(number, key_cap) + 1):
        if number % candidate == 0:
            pages_tile = candidate
    tile_owners = page_prefix.reshape(number // pages_tile, pages_tile)
    page_tiles = page_piece.reshape(
        number // pages_tile, pages_tile, 2, page_rows, head_count, head_width
    )

    def absorb_tile(current, tile_item):
        one_tile, tile_owner = tile_item
        tile_keys = one_tile[:, 0].reshape(pages_tile * page_rows, head_count, head_width)
        tile_values = one_tile[:, 1].reshape(pages_tile * page_rows, head_count, head_width)
        key_prefix = jnp.repeat(tile_owner, page_rows)
        allowed = token_prefix[:, None] == key_prefix[None, :]
        updated = absorb(current, queries, tile_keys, tile_values, allowed)
        return (updated, None)

    finished, ignored = lax.scan(absorb_tile, carried, (page_tiles, tile_owners))
    running_max, denominator, numerator = finished
    attention = (numerator / denominator[..., None]).astype(jnp.bfloat16)
    expert_count = out_proj.shape[0]
    expert_ids = jnp.arange(expert_count, dtype=jnp.int32)
    gate_table = jnp.where(
        att_experts[:, :, None] == expert_ids[None, None, :], att_gates[:, :, None], 0.0
    )
    combined = jnp.zeros((expert_count, tok_count, head_count, head_width), jnp.float32)
    for slot_index in range(slot_count):
        combined = (
            combined
            + gate_table[:, slot_index, :].T[:, :, None, None]
            * attention[:, :, slot_index, :].astype(jnp.float32)[None]
        )
    combined = combined.reshape(expert_count, tok_count, head_count * head_width).astype(
        jnp.bfloat16
    )
    column_sums = jnp.einsum(
        "etf,ecf->tc",
        combined,
        lax.all_gather(out_proj, "blk", axis=1, tiled=True),
        preferred_element_type=jnp.float32,
    )
    return lax.psum_scatter(column_sums.astype(jnp.bfloat16), "kv", scatter_dimension=1, tiled=True)


EARLY = 1
MESH = pl.DeviceIdType.MESH
F32 = jnp.float32
BF16 = jnp.bfloat16
NT = (((1,), (1,)), ((), ()))


def fused_kernel(
    pt_ref, rp_ref, sl_ref, ex_ref, ga_ref, q_ref, s_ref, c_ref, w_ref, o_ref,
    cbuf, wbuf, ubuf, tbl, bias, comb, pbuf, prec, fin,
    loc_sem, cz_send, cz_recv, cy_send, cy_recv, w_send, w_recv,
    t_send, t_recv, u_send, u_recv, p_send, p_recv, o_send, o_recv,
):
    blk = lax.axis_index("blk")
    k = lax.axis_index("kv")
    z = blk // 2
    y = blk % 2
    heads = 4
    tok = q_ref.shape[0]
    cached = cbuf.shape[0] * cbuf.shape[1] * cbuf.shape[3]
    page_rows = cbuf.shape[3]
    pages = pt_ref.shape[0]
    reqs = rp_ref.shape[0]
    partner = z * 2 + (1 - y)

    def zpeer(d):
        return lax.rem(z + d, 4)

    barrier = pltpu.get_barrier_semaphore()
    for dz in range(4):
        for dk in range(4):
            if dz or dk:
                pl.semaphore_signal(
                    barrier, inc=1, device_id=(zpeer(dz) * 2 + y, lax.rem(k + dk, 4)), device_id_type=MESH
                )
    pl.semaphore_signal(barrier, inc=1, device_id=(partner, k), device_id_type=MESH)
    pl.semaphore_wait(barrier, 16)

    def remote(src, dst, send, recv, to):
        return pltpu.make_async_remote_copy(
            src_ref=src, dst_ref=dst, send_sem=send, recv_sem=recv, device_id=to, device_id_type=MESH
        )

    def cz(d, slot):
        return remote(c_ref, cbuf.at[slot], cz_send.at[d - 1], cz_recv.at[d - 1], (zpeer(d) * 2 + y, k))

    def cy(d):
        slot = lax.rem(z - d + 4, 4) * 2 + y
        source = c_ref if d == 0 else cbuf.at[slot]
        return remote(source, cbuf.at[slot], cy_send.at[d], cy_recv.at[d], (partner, k))

    for d in (1, 3, 2):
        cz(d, blk).start()
    cy(0).start()
    own_c = pltpu.make_async_copy(c_ref, cbuf.at[blk], loc_sem.at[0])
    own_c.start()
    own_w = pltpu.make_async_copy(w_ref, wbuf.at[0], loc_sem.at[1])
    own_w.start()

    def wcopy(e):
        return remote(w_ref.at[e], wbuf.at[1, e], w_send.at[e], w_recv.at[e], (partner, k))

    for e in range(EARLY):
        wcopy(e).start()

    expert = lax.broadcasted_iota(jnp.int32, (8, tok), 0)
    for j in range(2):
        tbl[z, j * 8 : (j + 1) * 8] = jnp.where(expert == ex_ref[j : j + 1, :], 1.0, 0.0).astype(BF16)
    gates = [jnp.broadcast_to(ga_ref[j : j + 1, :], (128, tok)).T for j in range(2)]

    def tcopy(d, slot):
        return remote(tbl.at[slot], tbl.at[slot], t_send.at[d - 1], t_recv.at[d - 1], (zpeer(d) * 2 + y, k))

    row = lax.broadcasted_iota(jnp.int32, (tok, 128), 0)
    colq = lax.broadcasted_iota(jnp.int32, (8, tok), 1)
    req_row = jnp.zeros((tok, 128), jnp.int32)
    req_col = jnp.zeros((8, tok), jnp.int32)
    pref_row = jnp.full((tok, 128), rp_ref[0], jnp.int32)
    end = jnp.int32(0)
    for r in range(reqs):
        end = end + sl_ref[0, r]
        past = row >= end
        req_row = req_row + jnp.where(past, 1, 0)
        req_col = req_col + jnp.where(colq >= end, 1, 0)
        if r + 1 < reqs:
            pref_row = jnp.where(past, rp_ref[r + 1], pref_row)
    page_of = lax.broadcasted_iota(jnp.int32, (8, cached), 1) // page_rows
    key_prefix = jnp.zeros((8, cached), jnp.int32)
    for entry in range(pages):
        key_prefix = jnp.where(page_of == pt_ref[entry], entry // (pages // PREFIXES), key_prefix)
    bias[:, 0:cached] = jnp.where(pref_row[:, 0:1] == key_prefix[0:1, :], 0.0, MASKED_SCORE)
    keep = jnp.logical_and(req_row[:, 0:1] == req_col[0:1, :], row[:, 0:1] >= colq[0:1, :])
    bias[:, cached:] = jnp.where(keep, 0.0, MASKED_SCORE)

    own_c.wait()
    for d in (1, 3, 2):
        slot = lax.rem(z - d + 4, 4) * 2 + y
        cz(d, slot).wait_recv()
        cy(d).start()
    for e in range(EARLY, 8):
        wcopy(e).start()
    for d in (1, 2, 3):
        tcopy(d, z).start()
    for d in (0, 1, 3, 2):
        slot = lax.rem(z - d + 4, 4) * 2 + (1 - y)
        remote(cbuf.at[slot], cbuf.at[slot], cy_send.at[d], cy_recv.at[d], (partner, k)).wait_recv()

    def ulink(way, source, h):
        to = z + 1 - 2 * way
        return remote(
            ubuf.at[source, h], ubuf.at[source, h], u_send.at[way, source, h], u_recv.at[source, h], (to * 2 + y, k)
        )

    inner = jnp.logical_and(z > 0, z < 3)

    def pass_on(h):
        @pl.when(inner)
        def _():
            ulink(0, z - 1, h).wait_recv()
            ulink(0, z - 1, h).start()
            ulink(1, z + 1, h).wait_recv()
            ulink(1, z + 1, h).start()

    factor = math.log2(math.e) / math.sqrt(128)
    for h in range(heads):
        span = slice(h * 128, (h + 1) * 128)
        keys = cbuf[:, :, 0, :, span].reshape(cached, 128)
        values = cbuf[:, :, 1, :, span].reshape(cached, 128)
        skeys = s_ref[:, span]
        svalues = s_ref[:, heads * 128 + h * 128 : heads * 128 + (h + 1) * 128]
        for j in range(2):
            query = q_ref[:, (h * 2 + j) * 128 : (h * 2 + j + 1) * 128]
            sa = lax.dot_general(query, keys, NT, preferred_element_type=F32) * factor + bias[:, 0:cached]
            sb = lax.dot_general(query, skeys, NT, preferred_element_type=F32) * factor + bias[:, cached:]
            top = jnp.maximum(jnp.max(sa, axis=1, keepdims=True), jnp.max(sb, axis=1, keepdims=True))
            pa = jnp.exp2(sa - top)
            pb = jnp.exp2(sb - top)
            den = jnp.sum(pa, axis=1, keepdims=True) + jnp.sum(pb, axis=1, keepdims=True)
            num = jnp.dot(pa.astype(BF16), values, preferred_element_type=F32) + jnp.dot(
                pb.astype(BF16), svalues, preferred_element_type=F32
            )
            att = (num / den).astype(BF16).astype(F32)
            ubuf[z, h, :, j * 128 : (j + 1) * 128] = (att * gates[j]).astype(BF16)

        @pl.when(z < 3)
        def _():
            ulink(0, z, h).start()

        @pl.when(z > 0)
        def _():
            ulink(1, z, h).start()

        if h > 0:
            pass_on(h - 1)
    own_w.wait()

    sel_row = lax.broadcasted_iota(jnp.int32, (16, 16 * 128), 0)
    sel_col = lax.broadcasted_iota(jnp.int32, (16, 16 * 128), 1) // 128
    select = jnp.where(sel_row == sel_col, 1.0, 0.0).astype(BF16)

    def source_of(i):
        near = jnp.where(z < 2, z, 3 - z)
        later = jnp.where(near == 0, i, i - 1 + i // 2)
        base = jnp.where(i == 0, near, jnp.where(i == 3, 3, later))
        return jnp.where(z < 2, base, 3 - base)

    def pcopy(i, e):
        q = lax.rem(k + e, 4)
        rows = pl.ds(pl.multiple_of(q * 64, 64), 64)
        return remote(
            pbuf.at[i, rows], prec.at[i, e - 1], p_send.at[i, e - 1], p_recv.at[i, e - 1], (blk, q)
        )

    def block_at(i):
        return jnp.where(i < 6, lax.rem(i, 3), 3)

    def side_at(i):
        return jnp.where(i < 6, i // 3, i - 6)

    def half_of(side):
        half = jnp.where(side == 0, y, 1 - y)
        return pl.ds(pl.multiple_of(half * 256, 256), 256)

    def ocopy(i):
        d = block_at(i)
        rows = pl.ds(pl.multiple_of(k * 64, 64), 64)
        to = source_of(d) * 2 + y
        return remote(fin.at[i], o_ref.at[rows, half_of(side_at(i))], o_send.at[i], o_recv.at[side_at(i), k], (to, z))

    def step(i, carry):
        @pl.when(i < 8)
        def _():
            d = block_at(i)
            side = side_at(i)
            source = source_of(d)

            @pl.when(side == 0)
            def _():
                @pl.when(d == 1)
                def _():
                    pass_on(heads - 1)
                    for t in (1, 2, 3):
                        tcopy(t, z).wait_recv()

                @pl.when(jnp.logical_and(d > 0, jnp.logical_not(inner)))
                def _():
                    for h in range(heads):
                        remote(
                            ubuf.at[source, h], ubuf.at[source, h], u_send.at[0, source, h], u_recv.at[source, h], (blk, k)
                        ).wait_recv()

                mask = lax.dot_general(
                    tbl[source], select, (((0,), (0,)), ((), ())), preferred_element_type=F32
                ).astype(BF16)
                for h in range(heads):
                    u0 = ubuf[source, h, :, 0:128]
                    u1 = ubuf[source, h, :, 128:256]
                    for e in range(8):
                        comb[d, :, e * 512 + h * 128 : e * 512 + (h + 1) * 128] = (
                            u0 * mask[:, e * 128 : (e + 1) * 128] + u1 * mask[:, (8 + e) * 128 : (9 + e) * 128]
                        )

            @pl.when(jnp.logical_and(i == 3, inner))
            def _():
                for h in range(heads):
                    ulink(z % 2, source_of(3), h).wait_recv()
                    ulink(z % 2, source_of(3), h).start()

            @pl.when(i == 3)
            def _():
                for e in range(8):
                    wcopy(e).wait_recv()

            part = jnp.zeros((tok, 256), F32)
            for e in range(8):
                part = part + lax.dot_general(
                    comb[d, :, e * 512 : (e + 1) * 512], wbuf[side, e], NT, preferred_element_type=F32
                )
            pbuf[i] = part.astype(BF16)
            for e in (2, 3, 1):
                pcopy(i, e).start()

        @pl.when(i > 0)
        def _():
            p = i - 1
            own = pl.ds(pl.multiple_of(k * 64, 64), 64)
            total = pbuf[p, own].astype(F32)
            for e in (1, 2, 3):
                pcopy(p, e).wait_recv()
                total = total + prec[p, e - 1].astype(F32)
            here = jnp.logical_and(block_at(p) == 0, k == z)

            @pl.when(here)
            def _():
                o_ref[own, half_of(side_at(p))] = total.astype(BF16)

            @pl.when(jnp.logical_not(here))
            def _():
                fin[p] = total.astype(BF16)
                ocopy(p).start()

        return carry

    lax.fori_loop(0, 9, step, 0)

    for g in range(2):
        for q in range(4):
            rows = pl.ds(q * 64, 64)

            @pl.when(jnp.logical_or(k != z, k != q))
            def _():
                remote(
                    fin.at[0], o_ref.at[rows, half_of(g)], o_send.at[0], o_recv.at[g, q], (blk, k)
                ).wait_recv()

    def drain(i, carry):
        for e in (1, 2, 3):
            pcopy(i, e).wait_send()

        @pl.when(jnp.logical_or(block_at(i) != 0, k != z))
        def _():
            ocopy(i).wait_send()

        return carry

    lax.fori_loop(0, 8, drain, 0)
    for d in (1, 2, 3):
        cz(d, blk).wait_send()
        tcopy(d, z).wait_send()
    for d in range(4):
        cy(d).wait_send()
    for e in range(8):
        wcopy(e).wait_send()
    for h in range(heads):

        @pl.when(z < 3)
        def _():
            ulink(0, z, h).wait_send()

        @pl.when(z > 0)
        def _():
            ulink(1, z, h).wait_send()

        @pl.when(inner)
        def _():
            ulink(0, z - 1, h).wait_send()
            ulink(1, z + 1, h).wait_send()
            ulink(z % 2, source_of(3), h).wait_send()


def fused_body(
    queries, suffix_kv, cache, page_table, req_prefix, suffix_len, att_experts, att_gates, out_proj
):
    tok, heads, slots, width = queries.shape
    local_pages, _, page_rows = cache.shape[:3]
    experts, columns, features = out_proj.shape
    vmem = pl.BlockSpec(memory_space=pltpu.VMEM)
    smem = pl.BlockSpec(memory_space=pltpu.SMEM)
    dma = pltpu.SemaphoreType.DMA
    return pl.pallas_call(
        fused_kernel,
        out_shape=jax.ShapeDtypeStruct((tok, 2 * columns), BF16),
        in_specs=[smem, smem, smem, vmem, vmem, vmem, vmem, vmem, pl.BlockSpec(memory_space=pl.ANY)],
        out_specs=vmem,
        scratch_shapes=[
            pltpu.VMEM((8, local_pages, 2, page_rows, heads * width), BF16),
            pltpu.VMEM((2, experts, columns, features), BF16),
            pltpu.VMEM((4, heads, tok, slots * width), BF16),
            pltpu.VMEM((4, slots * experts, tok), BF16),
            pltpu.VMEM((tok, 8 * local_pages * page_rows + tok), F32),
            pltpu.VMEM((4, tok, experts * features), BF16),
            pltpu.VMEM((8, tok, columns), BF16),
            pltpu.VMEM((8, 3, tok // 4, columns), BF16),
            pltpu.VMEM((8, tok // 4, columns), BF16),
            dma((2,)), dma((3,)), dma((3,)), dma((4,)), dma((4,)), dma((experts,)), dma((experts,)),
            dma((3,)), dma((3,)), dma((2, 4, heads)), dma((4, heads)),
            dma((8, 3)), dma((8, 3)), dma((8,)), dma((2, 4)),
        ],
        compiler_params=pltpu.CompilerParams(
            collective_id=0, has_side_effects=True, vmem_limit_bytes=48 * 1024 * 1024
        ),
        cost_estimate=pl.CostEstimate(flops=6 * 10**9, bytes_accessed=8 * 10**6, transcendentals=2 * 10**6),
    )(
        page_table, req_prefix, suffix_len, att_experts.T, att_gates.T,
        queries.reshape(tok, heads * slots * width),
        suffix_kv.reshape(tok, 2 * heads * width),
        cache.reshape(local_pages, 2, page_rows, heads * width),
        out_proj,
    )


def solution(mesh):
    in_specs = (
        P("blk", "kv", None, None),
        P("blk", None, "kv", None),
        P("blk", None, None, "kv", None),
        P(),
        P("blk"),
        P("blk", None),
        P("blk", None),
        P("blk", None),
        P(None, "blk", "kv"),
    )
    out_specs = P("blk", "kv")
    chosen = body
    if mesh.shape["blk"] == 2 * mesh.shape["kv"] and mesh.shape["kv"] == 4:
        chosen = fused_body
    return jax.shard_map(chosen, mesh=mesh, in_specs=in_specs, out_specs=out_specs, check_vma=False)
```
